128 devices in a mesh: mem: 8 (over y, core), item: 16 (over z, x).
Axes of the slice: x: 4, y: 4, z: 4, core: 2. Of those that a mesh axis runs over, the one named last changes fastest.
Arguments:
- value_tiles: bfloat16 [16384, 256, 256], P(('mem', 'item')), may hold values from 0 to 1
- member_usage: float32 [8, 524288], P(None, ('mem', 'item')), may hold values from 0.002 to 0.02
- item_duals: float32 [8, 262144], P(None, ('mem', 'item')), may hold values from 1 to 10
- capacity: float32 [8, 262144], P(None, ('mem', 'item')), may hold values from 4 to 20
- tile_slot: int32 [16384], P(('mem', 'item')), may hold values from 0 to 127, as said below
- slot_item: int32 [16384], P(('mem', 'item')), may hold values from -1 to 1023, as said below
- real_tile_count: int32 [128], P(('mem', 'item')), may hold values from 32 to 128, as said below
- tile_member: int32 [16384], P(('mem', 'item')), may hold values from 0 to 15
Outputs:
- final_duals: float32 [8, 262144], P(None, ('mem', 'item'))
- item_slack: float32 [8, 262144], P(None, ('mem', 'item'))
- member_value: float32 [524288], P(('mem', 'item'))
The draws below stay inside these ranges and needn't reach their ends.
Inputs may be any that keep to these rules, and one draw needn't show every extreme that they name: `tile_slot`: slot o + c is the c-th of the 1 slots that a device sends to owner device o; every tile's slot is live (its slot_item is not -1). `slot_item`: per device, the live slots toward owner o name distinct item blocks among o * 8 to (o + 1) * 8 - 1; one owner receives at most 1 live slot from each device. `real_tile_count`: the real tiles of a device are its first ones; some device has all 128 real.
All inputs are finite; a program needn't handle non-finite values.
Results may differ from the reference program's by a relative error of at most 0.0003.
Values sent between devices are 32-bit elements; how exact they have to be, the bound alone decides.
A program may use at most 128 MiB of HBM per device.

```python
import math
import jax
import jax.numpy as jnp
from jax import lax

FAM = 8
TB = 256
CAP = 1
ITERS = 2
TILES_DEV = 128
MB_DEV = 16
IB_DEV = 8
SLOTS = 128
TILES = 16384
NB = 1024
ITEMS = 262144
MEMBERS = 524288
DEVICES = 128


def pattern(key):
    subkeys = jax.random.split(key, 6)
    slot_total = DEVICES * CAP
    shared_owner = jax.random.randint(subkeys[0], (), 0, DEVICES).astype(jnp.int32)
    full_device = jax.random.randint(subkeys[1], (), 0, DEVICES).astype(jnp.int32)
    divisors = jax.random.randint(subkeys[2], (DEVICES,), 1, 5).astype(jnp.int32)
    counts = (TILES_DEV // divisors).astype(jnp.int32)
    counts = jnp.where(jnp.arange(DEVICES, dtype=jnp.int32) == full_device, TILES_DEV, counts).astype(jnp.int32)
    used_slots = jnp.minimum(slot_total, jnp.maximum(CAP, counts * 7 // 8)).astype(jnp.int32)

    def owner_order(subkey):
        remaining = jax.random.permutation(subkey, DEVICES - 1).astype(jnp.int32) + 1
        return jnp.concatenate([jnp.zeros((1,), jnp.int32), remaining])
    owners = (jax.vmap(owner_order)(jax.random.split(subkeys[3], DEVICES)) + shared_owner) % DEVICES
    slot_order = (owners[:, :, None] * CAP + jnp.arange(CAP, dtype=jnp.int32)[None, None, :]).reshape(DEVICES, slot_total).astype(jnp.int32)
    slot_positions = jnp.arange(TILES_DEV, dtype=jnp.int32)[None, :] % used_slots[:, None]
    tile_slot = jnp.take_along_axis(slot_order, slot_positions, axis=1).astype(jnp.int32)
    slot_rank = jnp.argsort(slot_order, axis=1).astype(jnp.int32)
    is_live = slot_rank < used_slots[:, None]

    def offsets(subkey):
        return jax.random.permutation(subkey, IB_DEV)[:CAP].astype(jnp.int32)
    picked = jax.vmap(offsets)(jax.random.split(subkeys[4], DEVICES * DEVICES)).reshape(DEVICES, slot_total)
    owner_of_slot = jnp.arange(slot_total, dtype=jnp.int32) // CAP
    slot_item = jnp.where(is_live, owner_of_slot[None, :] * IB_DEV + picked, -1).astype(jnp.int32)
    tile_member = jax.random.randint(subkeys[5], (DEVICES, TILES_DEV), 0, MB_DEV).astype(jnp.int32)
    return (tile_slot.reshape(-1), slot_item.reshape(-1), counts, tile_member.reshape(-1))


def draw_tile_slot(key, part):
    return pattern(key)[0]


def draw_slot_item(key, part):
    return pattern(key)[1]


def draw_real_tile_count(key, part):
    return pattern(key)[2]


def draw_tile_member(key, part):
    return pattern(key)[3]


def levels(key, extent, cuts, smallest, top_value):
    factor_of = 1.0
    for dim, parts in cuts:
        steps = jax.random.uniform(jax.random.fold_in(jax.random.fold_in(key, 6), dim), (parts,), jnp.float32, smallest / len(cuts), top_value / len(cuts))
        factor_of = factor_of * jnp.repeat(jnp.exp(steps), extent[dim] // parts).reshape((-1,) + (1,) * (len(extent) - 1 - dim))
    return factor_of


def setup_inputs(seed: int = 0) -> dict:
    key_of = jax.random.split(jax.random.key(seed), 9)
    return {
        "value_tiles": jnp.clip(1.0 * jax.random.uniform(key_of[0], (TILES, TB, TB), jnp.float32) ** levels(key_of[0], (TILES, TB, TB), ((0, 128),), -0.2, 0.2), 0.0, 1.0).astype(jnp.bfloat16),
        "member_usage": jnp.clip(jnp.exp(math.log(0.02) - 2.30258502 * jax.random.uniform(key_of[1], (FAM, MEMBERS), jnp.float32) ** levels(key_of[1], (FAM, MEMBERS), ((1, 128),), -0.2, 0.2)), 0.002, 0.02),
        "item_duals": jnp.clip(jnp.exp(math.log(10.0) - 2.3025851 * jax.random.uniform(key_of[2], (FAM, ITEMS), jnp.float32) ** levels(key_of[2], (FAM, ITEMS), ((1, 128),), -0.2, 0.2)), 1.0, 10.0),
        "capacity": jnp.clip(4.0 + 16.0 * jax.random.uniform(key_of[3], (FAM, ITEMS), jnp.float32) ** levels(key_of[3], (FAM, ITEMS), ((1, 128),), -0.2, 0.2), 4.0, 20.0),
        "tile_slot": draw_tile_slot(jax.random.fold_in(key_of[8], 71), 0),
        "slot_item": draw_slot_item(jax.random.fold_in(key_of[8], 71), 0),
        "real_tile_count": draw_real_tile_count(jax.random.fold_in(key_of[8], 71), 0),
        "tile_member": draw_tile_member(jax.random.fold_in(key_of[8], 71), 0),
    }


smoothing = 0.5
ascent_rate = 0.05


def tile_pass(value_tiles, usage_tiles, panel_tiles):
    count_all = value_tiles.shape[0]
    tile_width = value_tiles.shape[1]
    families = usage_tiles.shape[1]
    blocking = math.gcd(count_all, 32)
    groups = count_all // blocking

    def single(operands):
        value_block, usage_block, panel_block = operands
        charged = jnp.einsum("tkm,tkj->tmj", usage_block, panel_block, precision=lax.Precision.HIGHEST)
        dense_values = value_block.astype(jnp.float32)
        chosen = jnp.clip((dense_values - charged) / smoothing, 0.0, 1.0)
        tile_load_values = jnp.einsum("tkm,tmj->tkj", usage_block, chosen, precision=lax.Precision.HIGHEST)
        worths = jnp.sum(dense_values * chosen, axis=2) / tile_width
        return tile_load_values, worths

    shaped = (value_tiles.reshape(groups, blocking, tile_width, tile_width),
              usage_tiles.reshape(groups, blocking, families, tile_width),
              panel_tiles.reshape(groups, blocking, families, tile_width))
    tile_load_values, worths = lax.map(single, shaped)
    return tile_load_values.reshape(count_all, families, tile_width), worths.reshape(count_all, tile_width)


def reference(value_tiles, member_usage, item_duals, capacity, tile_slot, slot_item, real_tile_count, tile_member):
    dual_blocks = item_duals.reshape(FAM, NB, TB)
    limit_blocks = capacity.reshape(FAM, NB, TB)
    dev_values = value_tiles.reshape(DEVICES, TILES_DEV, TB, TB)
    dev_usage = member_usage.reshape(FAM, DEVICES, MB_DEV, TB).transpose(1, 2, 0, 3)
    dev_slots = tile_slot.reshape(DEVICES, TILES_DEV)
    dev_items = slot_item.reshape(DEVICES, SLOTS)
    dev_members = tile_member.reshape(DEVICES, TILES_DEV)
    slot_positions = jnp.arange(TILES_DEV, dtype=jnp.int32)
    member_numbers = jnp.arange(MB_DEV, dtype=jnp.int32)

    def one_pass(current):
        panels_all = current.transpose(1, 0, 2)

        def per_device(running_total, inputs):
            value_d, usage_d, slot_d, items_d, device_count_array, member_device_rows = inputs
            block_numbers = items_d[slot_d].astype(jnp.int32)
            live_flags = (slot_positions < device_count_array).astype(jnp.float32)
            tile_load_values, worths = tile_pass(value_d, usage_d[member_device_rows], panels_all[block_numbers])
            running_total = running_total.at[block_numbers].add(tile_load_values * live_flags[:, None, None])
            member_lookup = (member_device_rows[None, :] == member_numbers[:, None]).astype(jnp.float32) * live_flags[None, :]
            worth_rows = jnp.dot(member_lookup, worths, precision=lax.Precision.HIGHEST)
            return running_total, worth_rows.reshape(MB_DEV * TB)

        running_total, worth_rows = lax.scan(
            per_device, jnp.zeros((NB, FAM, TB), jnp.float32),
            (dev_values, dev_usage, dev_slots, dev_items, real_tile_count, dev_members))
        return running_total.transpose(1, 0, 2), worth_rows.reshape(MEMBERS)

    for iteration in range(ITERS):
        item_load, member_value = one_pass(dual_blocks)
        slack_blocks = item_load - limit_blocks
        dual_blocks = jnp.maximum(dual_blocks + ascent_rate * slack_blocks, 0.0)
    return dual_blocks.reshape(FAM, ITEMS), slack_blocks.reshape(FAM, ITEMS), member_value
```

```python
import functools

import jax
import jax.numpy as jnp
from jax import lax
from jax.experimental import pallas as pl
from jax.experimental.pallas import tpu as pltpu
from jax.sharding import PartitionSpec as P

MESH = pl.DeviceIdType.MESH
F32 = jnp.float32
BF16 = jnp.bfloat16

ITERS = 2
TILES = 128
WIDTH = 256
HALF = 128
FAMILIES = 8
BLOCKS = 8
MEMBER_BLOCKS = 16
ITEM_AXIS = 16
CHIPS = 64
GROUP = 16
MEMBER_GROUP = 8
ascent_rate = 0.05


def split(values):
    high = values.astype(BF16)
    low = (values - high.astype(F32)).astype(BF16)
    return high, low


def kernel(
    order_ref, panel_ref, member_ref, last_ref, keep_ref, live_ref,
    value_hbm, usage_ref, duals_ref, capacity_ref, slots_ref,
    final_ref, slack_ref, worth_ref,
    values, left, right, duals, limits, requests, wanted,
    dual_out, dual_in_0a, dual_in_0b, dual_in_1a, dual_in_1b, load_out, load_in, prefix, partial, partner, worths,
    value_sem, request_sem, want_sem, request_send, pair_send, pair_recv,
    dual_send, dual_recv, load_send, load_recv,
):
    dual_in = ((dual_in_0a, dual_in_0b), (dual_in_1a, dual_in_1b))
    mem = lax.axis_index("mem")
    item = lax.axis_index("item")
    core = lax.rem(mem, 2)
    chip = lax.div(mem, 2) * ITEM_AXIS + item
    other = (mem + 1 - 2 * core, item)

    def place(step):
        to = lax.rem(chip + step, CHIPS)
        return to, (lax.div(to, ITEM_AXIS) * 2 + core, lax.rem(to, ITEM_AXIS))

    value_copy = pltpu.make_async_copy(value_hbm, values, value_sem)
    value_copy.start()

    barrier = pltpu.get_barrier_semaphore()

    def greet(step, carry):
        pl.semaphore_signal(barrier, inc=1, device_id=place(step)[1], device_id_type=MESH)
        return carry

    lax.fori_loop(1, CHIPS, greet, 0)
    pl.semaphore_signal(barrier, inc=1, device_id=other, device_id_type=MESH)

    for b in range(BLOCKS):
        for h in range(2):
            columns = pl.ds(b * WIDTH + h * HALF, HALF)
            duals[core, h, b] = duals_ref[:, columns]
            limits[core, h, b] = capacity_ref[:, columns]
    for b in range(MEMBER_BLOCKS):
        usage = usage_ref[:, b * WIDTH : (b + 1) * WIDTH]
        high, low = split(usage)
        stacked = jnp.concatenate([high, high, low, low], axis=0).astype(F32)
        left[b, :, 0:32] = stacked.T.astype(BF16)
        right[b] = jnp.concatenate([high * 2, low * 2], axis=0)

    pl.semaphore_wait(barrier, CHIPS)

    def ask(step, carry):
        to, device = place(step)
        pltpu.make_async_remote_copy(
            src_ref=slots_ref, dst_ref=requests.at[chip], send_sem=request_send,
            recv_sem=request_sem, device_id=device, device_id_type=MESH,
        ).start()
        return carry

    lax.fori_loop(1, CHIPS, ask, 0)
    pairs = [
        pltpu.make_async_remote_copy(
            src_ref=array.at[core], dst_ref=array.at[core], send_sem=pair_send.at[n],
            recv_sem=pair_recv.at[n], device_id=other, device_id_type=MESH,
        )
        for n, array in enumerate((duals, limits))
    ]
    for copy in pairs:
        copy.start()
    requests[chip] = slots_ref[...]
    rest = requests.at[pl.ds(0, CHIPS - 1)]
    pltpu.make_async_copy(rest, rest, request_sem).wait()
    table = pltpu.make_async_copy(requests, wanted, want_sem)
    table.start()
    for copy in pairs:
        copy.wait()
    table.wait()

    owners = [(lax.div(mem, 2) * 2 + q) * ITEM_AXIS + item for q in range(2)]

    def want(of, q):
        return wanted[of, 0, owners[q]] - owners[q] * BLOCKS

    def duals_copy(it, h, step):
        to, device = place(step)
        return pltpu.make_async_remote_copy(
            src_ref=dual_out.at[it, h, to], dst_ref=dual_in[it][h].at[chip],
            send_sem=dual_send.at[it, h], recv_sem=dual_recv.at[it, h],
            device_id=device, device_id_type=MESH,
        )

    def loads_copy(it, h, step):
        to, device = place(step)
        return pltpu.make_async_remote_copy(
            src_ref=load_out.at[it, h, to], dst_ref=load_in.at[it, h, chip],
            send_sem=load_send.at[it, h], recv_sem=load_recv.at[it, h],
            device_id=device, device_id_type=MESH,
        )

    def pick(h, to, q):
        return duals[q, h, jnp.maximum(want(to, q), 0)]

    def send_duals(it, h):
        def one(step, carry):
            to, _ = place(step)
            for q in range(2):
                dual_out[it, h, to, q] = pick(h, to, q)
            duals_copy(it, h, step).start()
            return carry

        lax.fori_loop(1, CHIPS, one, 0)
        for q in range(2):
            dual_in[it][h][chip, q] = pick(h, chip, q)

    def send_load(it, h, step):
        to, _ = place(step)
        for q in range(2):
            load_out[it, h, to, q] = prefix[h, last_ref[to * 2 + q]]
        loads_copy(it, h, step).start()

    def keep_load(it, h):
        for q in range(2):
            load_in[it, h, chip, q] = prefix[h, last_ref[chip * 2 + q]]

    def send_loads(it, h, first):
        def one(step, carry):
            send_load(it, h, step)
            return carry

        lax.fori_loop(first, CHIPS, one, 0)
        keep_load(it, h)

    def arrived(ref, sem):
        rest = ref.at[pl.ds(0, CHIPS - 1)]
        pltpu.make_async_copy(rest, rest, sem).wait()

    def panel(it, h, slot):
        block = dual_in[it][h][slot // 2, slot % 2]
        high = block.astype(BF16).astype(F32)
        pair = jnp.concatenate([high, block - high], axis=0).astype(BF16)
        return jnp.concatenate([pair, pair], axis=0)

    def sweep(it, h, beside):
        def step(group, total):
            for n in range(GROUP):
                t = group * GROUP + n
                block = member_ref[t]
                charge = jnp.dot(
                    left[block, :, 0:32], panel(it, h, panel_ref[t]), preferred_element_type=F32
                )
                value = values[order_ref[t], :, h * HALF : (h + 1) * HALF].astype(F32)
                chosen = jnp.clip(value - charge, 0.0, 0.5)
                high, low = split(chosen)
                usage = right[block]
                load = jnp.dot(usage, high, preferred_element_type=F32) + jnp.dot(
                    usage, low, preferred_element_type=F32
                )
                load = load[0:FAMILIES] + load[FAMILIES:]
                total = total * keep_ref[t] + load * live_ref[t]
                prefix[h, t] = total
            if beside is not None:
                for n in range(7):
                    beside(1 + group * 7 + n)
            return total

        lax.fori_loop(0, TILES // GROUP, step, jnp.zeros((FAMILIES, HALF), F32))

    def gather_loads(it, h):
        arrived(load_in.at[it, h], load_recv.at[it, h])

        def one(step, sums):
            sums = list(sums)
            for n in range(2):
                of = step * 2 + n
                for q in range(2):
                    row = want(of, q)
                    piece = load_in[it, h, of, q]
                    for b in range(BLOCKS):
                        sums[q * BLOCKS + b] += jnp.where(row == b, piece, 0.0)
            return tuple(sums)

        zero = jnp.zeros((FAMILIES, HALF), F32)
        sums = lax.fori_loop(0, CHIPS // 2, one, (zero,) * (2 * BLOCKS))
        for q in range(2):
            for b in range(BLOCKS):
                partial[it, h, q, b] = sums[q * BLOCKS + b]

    def pair_copy(it, h):
        n = 2 + it * 2 + h
        return pltpu.make_async_remote_copy(
            src_ref=partial.at[it, h], dst_ref=partner.at[it, h], send_sem=pair_send.at[n],
            recv_sem=pair_recv.at[n], device_id=other, device_id_type=MESH,
        )

    def ascend(it, h):
        for q in range(2):
            for b in range(BLOCKS):
                slack = partial[it, h, q, b] + partner[it, h, q, b] - limits[q, h, b]
                duals[q, h, b] = jnp.maximum(duals[q, h, b] + ascent_rate * slack, 0.0)

    def finish(it, h):
        for b in range(BLOCKS):
            columns = pl.ds(b * WIDTH + h * HALF, HALF)
            slack = partial[it, h, core, b] + partner[it, h, core, b] - limits[core, h, b]
            slack_ref[:, columns] = slack
            final_ref[:, columns] = jnp.maximum(duals[core, h, b] + ascent_rate * slack, 0.0)

    def worth_sweep(it):
        worths[...] = jnp.zeros_like(worths)
        lanes = lax.broadcasted_iota(jnp.int32, (WIDTH, HALF), 1)

        def step(group, carry):
            total = worths[...]
            for n in range(MEMBER_GROUP):
                t = group * MEMBER_GROUP + n
                block = member_ref[t]
                slot = panel_ref[t]
                both = jnp.concatenate([panel(it, 0, slot), panel(it, 1, slot)], axis=1)
                charge = jnp.dot(left[block, :, 0:32], both, preferred_element_type=F32)
                value = values[order_ref[t]].astype(F32)
                worth = value * jnp.clip(value - charge, 0.0, 0.5)
                worth = jnp.sum(worth[:, :HALF] + worth[:, HALF:], axis=1, keepdims=True)
                total += jnp.where(lanes == block, worth * live_ref[t], 0.0)
            worths[...] = total
            return carry

        lax.fori_loop(0, TILES // MEMBER_GROUP, step, 0)
        rows = worths[...].T[0:MEMBER_BLOCKS] * (2.0 / WIDTH)
        for b in range(MEMBER_BLOCKS):
            for h in range(2):
                worth_ref[2 * b + h : 2 * b + h + 1, :] = rows[b : b + 1, h * HALF : (h + 1) * HALF]

    send_duals(0, 0)
    send_duals(0, 1)
    value_copy.wait()
    for it in range(ITERS):
        arrived(dual_in[it][0], dual_recv.at[it, 0])
        sweep(it, 0, None)
        arrived(dual_in[it][1], dual_recv.at[it, 1])
        sweep(it, 1, functools.partial(send_load, it, 0))
        send_loads(it, 0, 57)
        send_loads(it, 1, 1)
        if it == ITERS - 1:
            worth_sweep(it)
        for h in range(2):
            gather_loads(it, h)
            copy = pair_copy(it, h)
            copy.start()
            copy.wait()
            if it < ITERS - 1:
                ascend(it, h)
                send_duals(it + 1, h)
            else:
                finish(it, h)

    sent = requests.at[pl.ds(0, CHIPS - 1)]
    pltpu.make_async_copy(sent, sent, request_send).wait()
    for it in range(ITERS):
        for h in range(2):
            for ref, sem in ((dual_out, dual_send), (load_out, load_send)):
                arrived(ref.at[it, h], sem.at[it, h])


def on_device(
    value_tiles, member_usage, item_duals, capacity, tile_slot, slot_item, real_tile_count, tile_member
):
    places = jnp.arange(TILES, dtype=jnp.int32)
    slot = tile_slot // 32 * 32 + tile_slot % 16 * 2 + tile_slot // 16 % 2
    before = (slot[None, :] < slot[:, None]) | (
        (slot[None, :] == slot[:, None]) & (places[None, :] < places[:, None])
    )
    rank = jnp.sum(before.astype(jnp.int32), axis=1)
    at = (rank[:, None] == places[None, :]).astype(jnp.int32)
    order = jnp.sum(at * places[:, None], axis=0)
    panel = jnp.sum(at * slot[:, None], axis=0)
    member = jnp.sum(at * tile_member[:, None], axis=0)
    last = jnp.maximum(jnp.sum((slot[:, None] <= places[None, :]).astype(jnp.int32), axis=0) - 1, 0)
    keep = jnp.concatenate([jnp.zeros((1,), F32), (panel[1:] == panel[:-1]).astype(F32)])
    live = (order < real_tile_count[0]).astype(F32)

    smem = pl.BlockSpec(memory_space=pltpu.SMEM)
    vmem = pl.BlockSpec(memory_space=pltpu.VMEM)
    dma = pltpu.SemaphoreType.DMA
    blocks = (FAMILIES, HALF)
    final, slack, worth = pl.pallas_call(
        kernel,
        out_shape=(
            jax.ShapeDtypeStruct(item_duals.shape, F32),
            jax.ShapeDtypeStruct(item_duals.shape, F32),
            jax.ShapeDtypeStruct((2 * MEMBER_BLOCKS, HALF), F32),
        ),
        in_specs=[smem] * 6 + [pl.BlockSpec(memory_space=pl.ANY)] + [vmem] * 4,
        out_specs=(vmem,) * 3,
        scratch_shapes=[
            pltpu.VMEM((TILES, WIDTH, WIDTH), BF16),
            pltpu.VMEM((MEMBER_BLOCKS, WIDTH, HALF), BF16),
            pltpu.VMEM((MEMBER_BLOCKS, 2 * FAMILIES, WIDTH), BF16),
            pltpu.VMEM((2, 2, BLOCKS) + blocks, F32),
            pltpu.VMEM((2, 2, BLOCKS) + blocks, F32),
            pltpu.VMEM((CHIPS, 1, TILES), jnp.int32),
            pltpu.SMEM((CHIPS, 1, TILES), jnp.int32),
            pltpu.VMEM((ITERS, 2, CHIPS, 2) + blocks, F32),
            *[pltpu.VMEM((CHIPS, 2) + blocks, F32)] * (2 * ITERS),
            pltpu.VMEM((ITERS, 2, CHIPS, 2) + blocks, F32),
            pltpu.VMEM((ITERS, 2, CHIPS, 2) + blocks, F32),
            pltpu.VMEM((2, TILES) + blocks, F32),
            pltpu.VMEM((ITERS, 2, 2, BLOCKS) + blocks, F32),
            pltpu.VMEM((ITERS, 2, 2, BLOCKS) + blocks, F32),
            pltpu.VMEM((WIDTH, HALF), F32),
            dma, dma, dma, dma, dma((2 + 2 * ITERS,)), dma((2 + 2 * ITERS,)),
            dma((ITERS, 2)), dma((ITERS, 2)), dma((ITERS, 2)), dma((ITERS, 2)),
        ],
        compiler_params=pltpu.CompilerParams(
            collective_id=0, has_side_effects=True, vmem_limit_bytes=48 * 2**20
        ),
    )(
        order, panel, member, last, keep, live,
        value_tiles, member_usage, item_duals, capacity, slot_item.reshape(1, TILES),
    )
    return final, slack, worth.reshape(MEMBER_BLOCKS * WIDTH)


def solution(mesh):
    both = ("mem", "item")
    return jax.shard_map(
        on_device,
        mesh=mesh,
        in_specs=(
            P(both, None, None),
            P(None, both),
            P(None, both),
            P(None, both),
            P(both),
            P(both),
            P(both),
            P(both),
        ),
        out_specs=(P(None, both), P(None, both), P(both)),
        check_vma=False,
    )
```

```python
import functools

import jax
import jax.numpy as jnp
from jax import lax
from jax.experimental import pallas as pl
from jax.experimental.pallas import tpu as pltpu
from jax.sharding import PartitionSpec as P

MESH = pl.DeviceIdType.MESH
F32 = jnp.float32
BF16 = jnp.bfloat16

ITERS = 2
TILES = 128
WIDTH = 256
HALF = 128
FAMILIES = 8
BLOCKS = 8
MEMBER_BLOCKS = 16
ITEM_AXIS = 16
CHIPS = 64
GROUP = 16
MEMBER_GROUP = 8
ascent_rate = 0.05


def split(values):
    high = values.astype(BF16)
    low = (values - high.astype(F32)).astype(BF16)
    return high, low


def kernel(
    count_ref, value_hbm, usage_hbm, duals_hbm, capacity_hbm, slot_hbm, ask_hbm, member_hbm,
    final_ref, slack_ref, worth_ref,
    values, usage_ref, duals_ref, capacity_ref, slot_ref, slots_ref, place_ref, whole, parts, whole_smem, parts_smem,
    left, right, duals, limits, requests, wanted,
    dual_out, dual_in_0a, dual_in_0b, dual_in_1a, dual_in_1b, load_out, load_in, prefix, partial, partner, worths, asked,
    value_sem, input_sem, request_sem, want_sem, request_send, pair_send, pair_recv,
    dual_send, dual_recv, load_send, load_recv,
):
    dual_in = ((dual_in_0a, dual_in_0b), (dual_in_1a, dual_in_1b))
    mem = lax.axis_index("mem")
    item = lax.axis_index("item")
    core = lax.rem(mem, 2)
    chip = lax.div(mem, 2) * ITEM_AXIS + item
    other = (mem + 1 - 2 * core, item)

    def place(step):
        to = lax.rem(chip + step, CHIPS)
        return to, (lax.div(to, ITEM_AXIS) * 2 + core, lax.rem(to, ITEM_AXIS))

    barrier = pltpu.get_barrier_semaphore()

    def greet(step, carry):
        pl.semaphore_signal(barrier, inc=1, device_id=place(step)[1], device_id_type=MESH)
        return carry

    inputs = [
        pltpu.make_async_copy(source, target, input_sem.at[n])
        for n, (source, target) in enumerate((
            (ask_hbm, slots_ref), (duals_hbm, duals_ref), (capacity_hbm, capacity_ref),
            (usage_hbm, usage_ref), (slot_hbm, slot_ref), (member_hbm, place_ref),
        ))
    ]
    for copy in inputs:
        copy.start()
    value_copy = pltpu.make_async_copy(value_hbm, values, value_sem)
    value_copy.start()
    lax.fori_loop(1, CHIPS, greet, 0)
    pl.semaphore_signal(barrier, inc=1, device_id=other, device_id_type=MESH)

    for copy in inputs:
        copy.wait()
    for b in range(BLOCKS):
        for h in range(2):
            columns = pl.ds(b * WIDTH + h * HALF, HALF)
            duals[core, h, b] = duals_ref[:, columns]
            limits[core, h, b] = capacity_ref[:, columns]

    pl.semaphore_wait(barrier, CHIPS)

    def ask(step, carry):
        to, device = place(step)
        pltpu.make_async_remote_copy(
            src_ref=slots_ref, dst_ref=requests.at[chip], send_sem=request_send,
            recv_sem=request_sem, device_id=device, device_id_type=MESH,
        ).start()
        return carry

    lax.fori_loop(1, CHIPS, ask, 0)
    pairs = [
        pltpu.make_async_remote_copy(
            src_ref=array.at[core], dst_ref=array.at[core], send_sem=pair_send.at[n],
            recv_sem=pair_recv.at[n], device_id=other, device_id_type=MESH,
        )
        for n, array in enumerate((duals, limits))
    ]
    for copy in pairs:
        copy.start()
    requests[chip] = slots_ref[...]

    for b in range(MEMBER_BLOCKS):
        usage = usage_ref[:, b * WIDTH : (b + 1) * WIDTH]
        high, low = split(usage)
        stacked = jnp.concatenate([high, high, low, low], axis=0).astype(F32)
        left[b, :, 0:32] = stacked.T.astype(BF16)
        right[b] = jnp.concatenate([high * 2, low * 2], axis=0)

    rest = requests.at[pl.ds(0, CHIPS - 1)]
    pltpu.make_async_copy(rest, rest, request_sem).wait()
    table = pltpu.make_async_copy(requests, wanted, want_sem)
    table.start()
    for copy in pairs:
        copy.wait()
    table.wait()

    def sort_tiles():
        square = (TILES, TILES)
        down = lax.broadcasted_iota(jnp.int32, square, 0)
        across = lax.broadcasted_iota(jnp.int32, square, 1)

        def column(row):
            return jnp.broadcast_to(row, square).T

        def placed(chosen, numbers):
            return jnp.sum(jnp.where(chosen, numbers, 0), axis=0, keepdims=True)

        given = slot_ref[...]
        slot = given // 32 * 32 + given % 16 * 2 + given // 16 % 2
        slots = column(slot)
        before = (slots < slot) | ((slots == slot) & (down < across))
        rank = column(placed(before, 1))
        at = rank == across
        order = placed(at, down)
        panels = placed(at, slots)
        earlier = placed(rank == across - 1, slots)
        members = placed(at, column(place_ref[...]))
        last = jnp.maximum(placed(slots <= across, 1) - 1, 0)
        lane = lax.broadcasted_iota(jnp.int32, (1, TILES), 1)
        real = order < count_ref[0]
        counted = jnp.where(real, members, -1)
        whole[...] = jnp.zeros_like(whole)
        parts[...] = jnp.zeros_like(parts)
        for n, row in enumerate((order, panels, members, last, counted)):
            whole[n : n + 1, :] = row
        parts[0:1, :] = jnp.where((panels == earlier) & (lane > 0), 1.0, 0.0)
        parts[1:2, :] = jnp.where(real, 1.0, 0.0)
        tables = [
            pltpu.make_async_copy(source, target, input_sem.at[n])
            for n, (source, target) in enumerate(((whole, whole_smem), (parts, parts_smem)))
        ]
        for copy in tables:
            copy.start()
        for copy in tables:
            copy.wait()

    owners = [(lax.div(mem, 2) * 2 + q) * ITEM_AXIS + item for q in range(2)]

    def want(of, q):
        return wanted[of, 0, owners[q]] - owners[q] * BLOCKS

    def duals_copy(it, h, step):
        to, device = place(step)
        return pltpu.make_async_remote_copy(
            src_ref=dual_out.at[it, h, to], dst_ref=dual_in[it][h].at[chip],
            send_sem=dual_send.at[it, h], recv_sem=dual_recv.at[it, h],
            device_id=device, device_id_type=MESH,
        )

    def loads_copy(it, h, step):
        to, device = place(step)
        return pltpu.make_async_remote_copy(
            src_ref=load_out.at[it, h, to], dst_ref=load_in.at[it, h, chip],
            send_sem=load_send.at[it, h], recv_sem=load_recv.at[it, h],
            device_id=device, device_id_type=MESH,
        )

    def pick(h, to, q):
        return duals[q, h, jnp.maximum(want(to, q), 0)]

    def send_duals(it, h):
        def one(step, carry):
            send_dual(it, h, step)
            return carry

        lax.fori_loop(1, CHIPS, one, 0, unroll=3)
        keep_duals(it, h)

    def send_dual(it, h, step):
        to, _ = place(step)
        for q in range(2):
            dual_out[it, h, to, q] = pick(h, to, q)
        duals_copy(it, h, step).start()

    def keep_duals(it, h):
        for q in range(2):
            dual_in[it][h][chip, q] = pick(h, chip, q)

    def send_load(it, h, step):
        to, _ = place(step)
        for q in range(2):
            load_out[it, h, to, q] = prefix[h, whole_smem[3, to * 2 + q]]
        loads_copy(it, h, step).start()

    def keep_load(it, h):
        for q in range(2):
            load_in[it, h, chip, q] = prefix[h, whole_smem[3, chip * 2 + q]]

    def send_loads(it, h):
        def one(step, carry):
            send_load(it, h, step)
            return carry

        lax.fori_loop(1, CHIPS, one, 0, unroll=3)
        keep_load(it, h)

    def arrived(ref, sem):
        rest = ref.at[pl.ds(0, CHIPS - 1)]
        pltpu.make_async_copy(rest, rest, sem).wait()

    def panel(it, h, slot):
        block = dual_in[it][h][slot // 2, slot % 2]
        high = block.astype(BF16).astype(F32)
        pair = jnp.concatenate([high, block - high], axis=0).astype(BF16)
        return jnp.concatenate([pair, pair], axis=0)

    def sweep(it, h):
        def step(group, total):
            for n in range(GROUP):
                t = group * GROUP + n
                block = whole_smem[2, t]
                charge = jnp.dot(
                    left[block, :, 0:32], panel(it, h, whole_smem[1, t]), preferred_element_type=F32
                )
                value = values[whole_smem[0, t], :, h * HALF : (h + 1) * HALF].astype(F32)
                chosen = jnp.clip(value - charge, 0.0, 0.5)
                high, low = split(chosen)
                usage = right[block]
                load = jnp.dot(usage, high, preferred_element_type=F32) + jnp.dot(
                    usage, low, preferred_element_type=F32
                )
                load = load[0:FAMILIES] + load[FAMILIES:]
                total = total * parts_smem[0, t] + load * parts_smem[1, t]
                prefix[h, t] = total
            return total

        lax.fori_loop(0, TILES // GROUP, step, jnp.zeros((FAMILIES, HALF), F32))

    def note_asked():
        rows = lax.broadcasted_iota(jnp.int32, (BLOCKS, HALF), 0)

        def one(step, carry):
            for n in range(4):
                for q in range(2):
                    of = step * 4 + n
                    asked[of, q] = jnp.where(rows == want(of, q), 1.0, 0.0)
            return carry

        lax.fori_loop(0, CHIPS // 4, one, 0)

    def gather_loads(it, h):
        arrived(load_in.at[it, h], load_recv.at[it, h])

        def one(step, sums):
            sums = list(sums)
            for n in range(2):
                of = step * 2 + n
                for q in range(2):
                    piece = load_in[it, h, of, q]
                    for b in range(BLOCKS):
                        sums[q * BLOCKS + b] += piece * asked[of, q, b : b + 1, :]
            return tuple(sums)

        zero = jnp.zeros((FAMILIES, HALF), F32)
        sums = lax.fori_loop(0, CHIPS // 2, one, (zero,) * (2 * BLOCKS))
        for q in range(2):
            for b in range(BLOCKS):
                partial[it, h, q, b] = sums[q * BLOCKS + b]

    def pair_copy(it, h):
        n = 2 + it * 2 + h
        return pltpu.make_async_remote_copy(
            src_ref=partial.at[it, h], dst_ref=partner.at[it, h], send_sem=pair_send.at[n],
            recv_sem=pair_recv.at[n], device_id=other, device_id_type=MESH,
        )

    def ascend(it, h):
        for q in range(2):
            for b in range(BLOCKS):
                slack = partial[it, h, q, b] + partner[it, h, q, b] - limits[q, h, b]
                duals[q, h, b] = jnp.maximum(duals[q, h, b] + ascent_rate * slack, 0.0)

    def finish(it, h):
        for b in range(BLOCKS):
            columns = pl.ds(b * WIDTH + h * HALF, HALF)
            slack = partial[it, h, core, b] + partner[it, h, core, b] - limits[core, h, b]
            slack_ref[:, columns] = slack
            final_ref[:, columns] = jnp.maximum(duals[core, h, b] + ascent_rate * slack, 0.0)

    def worth_sweep(it):
        worths[...] = jnp.zeros_like(worths)
        lanes = lax.broadcasted_iota(jnp.int32, (WIDTH, HALF), 1)

        def step(group, carry):
            total = worths[...]
            for n in range(MEMBER_GROUP):
                t = group * MEMBER_GROUP + n
                block = whole_smem[2, t]
                slot = whole_smem[1, t]
                both = jnp.concatenate([panel(it, 0, slot), panel(it, 1, slot)], axis=1)
                charge = jnp.dot(left[block, :, 0:32], both, preferred_element_type=F32)
                value = values[whole_smem[0, t]].astype(F32)
                worth = value * jnp.clip(value - charge, 0.0, 0.5)
                worth = jnp.sum(worth[:, :HALF] + worth[:, HALF:], axis=1, keepdims=True)
                total += jnp.where(lanes == whole_smem[4, t], worth, 0.0)
            worths[...] = total
            return carry

        lax.fori_loop(0, TILES // MEMBER_GROUP, step, 0)
        rows = worths[...].T[0:MEMBER_BLOCKS] * (2.0 / WIDTH)
        for b in range(MEMBER_BLOCKS):
            for h in range(2):
                worth_ref[2 * b + h : 2 * b + h + 1, :] = rows[b : b + 1, h * HALF : (h + 1) * HALF]

    send_duals(0, 0)
    send_duals(0, 1)
    sort_tiles()
    note_asked()
    value_copy.wait()
    for it in range(ITERS):
        final = it == ITERS - 1
        for h in range(2):
            arrived(dual_in[it][h], dual_recv.at[it, h])
            sweep(it, h)
            if h == 0:
                send_loads(it, h)
        for h in range(2):
            gather_loads(it, h)
            copy = pair_copy(it, h)
            copy.start()
            if h == 0:
                send_loads(it, 1)
            copy.wait()
            if final:
                finish(it, h)
            else:
                ascend(it, h)
                send_duals(it + 1, h)
            if final and h == 0:
                worth_sweep(it)

    sent = requests.at[pl.ds(0, CHIPS - 1)]
    pltpu.make_async_copy(sent, sent, request_send).wait()
    for it in range(ITERS):
        for h in range(2):
            for ref, sem in ((dual_out, dual_send), (load_out, load_send)):
                arrived(ref.at[it, h], sem.at[it, h])


def on_device(
    value_tiles, member_usage, item_duals, capacity, tile_slot, slot_item, real_tile_count, tile_member
):
    vmem = pl.BlockSpec(memory_space=pltpu.VMEM)
    dma = pltpu.SemaphoreType.DMA
    blocks = (FAMILIES, HALF)
    final, slack, worth = pl.pallas_call(
        kernel,
        out_shape=(
            jax.ShapeDtypeStruct(item_duals.shape, F32),
            jax.ShapeDtypeStruct(item_duals.shape, F32),
            jax.ShapeDtypeStruct((2 * MEMBER_BLOCKS, HALF), F32),
        ),
        in_specs=[pl.BlockSpec(memory_space=pltpu.SMEM)] + [pl.BlockSpec(memory_space=pl.ANY)] * 7,
        out_specs=(vmem,) * 3,
        scratch_shapes=[
            pltpu.VMEM((TILES, WIDTH, WIDTH), BF16),
            pltpu.VMEM(member_usage.shape, F32),
            pltpu.VMEM(item_duals.shape, F32),
            pltpu.VMEM(item_duals.shape, F32),
            pltpu.VMEM((1, TILES), jnp.int32),
            pltpu.VMEM((1, TILES), jnp.int32),
            pltpu.VMEM((1, TILES), jnp.int32),
            pltpu.VMEM((8, TILES), jnp.int32),
            pltpu.VMEM((8, TILES), F32),
            pltpu.SMEM((8, TILES), jnp.int32),
            pltpu.SMEM((8, TILES), F32),
            pltpu.VMEM((MEMBER_BLOCKS, WIDTH, HALF), BF16),
            pltpu.VMEM((MEMBER_BLOCKS, 2 * FAMILIES, WIDTH), BF16),
            pltpu.VMEM((2, 2, BLOCKS) + blocks, F32),
            pltpu.VMEM((2, 2, BLOCKS) + blocks, F32),
            pltpu.VMEM((CHIPS, 1, TILES), jnp.int32),
            pltpu.SMEM((CHIPS, 1, TILES), jnp.int32),
            pltpu.VMEM((ITERS, 2, CHIPS, 2) + blocks, F32),
            *[pltpu.VMEM((CHIPS, 2) + blocks, F32)] * (2 * ITERS),
            pltpu.VMEM((ITERS, 2, CHIPS, 2) + blocks, F32),
            pltpu.VMEM((ITERS, 2, CHIPS, 2) + blocks, F32),
            pltpu.VMEM((2, TILES) + blocks, F32),
            pltpu.VMEM((ITERS, 2, 2, BLOCKS) + blocks, F32),
            pltpu.VMEM((ITERS, 2, 2, BLOCKS) + blocks, F32),
            pltpu.VMEM((WIDTH, HALF), F32),
            pltpu.VMEM((CHIPS, 2, BLOCKS, HALF), F32),
            dma, dma((6,)), dma, dma, dma, dma((2 + 2 * ITERS,)), dma((2 + 2 * ITERS,)),
            dma((ITERS, 2)), dma((ITERS, 2)), dma((ITERS, 2)), dma((ITERS, 2)),
        ],
        compiler_params=pltpu.CompilerParams(
            collective_id=0, has_side_effects=True, vmem_limit_bytes=64 * 2**20 - 2**18
        ),
    )(
        real_tile_count, value_tiles, member_usage, item_duals, capacity,
        tile_slot.reshape(1, TILES), slot_item.reshape(1, TILES), tile_member.reshape(1, TILES),
    )
    return final, slack, worth.reshape(MEMBER_BLOCKS * WIDTH)


def solution(mesh):
    both = ("mem", "item")
    return jax.shard_map(
        on_device,
        mesh=mesh,
        in_specs=(
            P(both, None, None),
            P(None, both),
            P(None, both),
            P(None, both),
            P(both),
            P(both),
            P(both),
            P(both),
        ),
        out_specs=(P(None, both), P(None, both), P(both)),
        check_vma=False,
    )
```

```python
import functools

import jax
import jax.numpy as jnp
from jax import lax
from jax.experimental import pallas as pl
from jax.experimental.pallas import tpu as pltpu
from jax.sharding import PartitionSpec as P

MESH = pl.DeviceIdType.MESH
F32 = jnp.float32
BF16 = jnp.bfloat16

ITERS = 2
TILES = 128
WIDTH = 256
HALF = 128
FAMILIES = 8
BLOCKS = 8
MEMBER_BLOCKS = 16
ITEM_AXIS = 16
CHIPS = 64
GROUP = 16
MEMBER_GROUP = 8
ascent_rate = 0.05


def split(values):
    high = values.astype(BF16)
    low = (values - high.astype(F32)).astype(BF16)
    return high, low


def kernel(
    count_ref, value_hbm, usage_hbm, duals_hbm, capacity_hbm, slot_hbm, ask_hbm, member_hbm,
    final_ref, slack_ref, worth_ref,
    values, usage_ref, duals_ref, capacity_ref, slot_ref, slots_ref, place_ref, whole, parts, whole_smem, parts_smem,
    left, right, duals, limits, requests, wanted,
    dual_out, dual_in_0a, dual_in_0b, dual_in_1a, dual_in_1b, load_out, load_in, prefix, partial, partner, worths, asked,
    value_sem, input_sem, request_sem, want_sem, request_send, pair_send, pair_recv,
    dual_send, dual_recv, load_send, load_recv,
):
    dual_in = ((dual_in_0a, dual_in_0b), (dual_in_1a, dual_in_1b))
    mem = lax.axis_index("mem")
    item = lax.axis_index("item")
    core = lax.rem(mem, 2)
    chip = lax.div(mem, 2) * ITEM_AXIS + item
    other = (mem + 1 - 2 * core, item)

    def place(step):
        to = lax.rem(chip + step, CHIPS)
        return to, (lax.div(to, ITEM_AXIS) * 2 + core, lax.rem(to, ITEM_AXIS))

    barrier = pltpu.get_barrier_semaphore()

    def greet(step, carry):
        pl.semaphore_signal(barrier, inc=1, device_id=place(step)[1], device_id_type=MESH)
        return carry

    inputs = [
        pltpu.make_async_copy(source, target, input_sem.at[n])
        for n, (source, target) in enumerate((
            (ask_hbm, slots_ref), (duals_hbm, duals_ref), (capacity_hbm, capacity_ref),
            (usage_hbm, usage_ref), (slot_hbm, slot_ref), (member_hbm, place_ref),
        ))
    ]
    lax.fori_loop(1, CHIPS, greet, 0, unroll=7)
    pl.semaphore_signal(barrier, inc=1, device_id=other, device_id_type=MESH)
    for copy in inputs:
        copy.start()
    value_copy = pltpu.make_async_copy(value_hbm, values, value_sem)
    value_copy.start()

    for copy in inputs:
        copy.wait()
    for b in range(BLOCKS):
        for h in range(2):
            columns = pl.ds(b * WIDTH + h * HALF, HALF)
            duals[core, h, b] = duals_ref[:, columns]
            limits[core, h, b] = capacity_ref[:, columns]

    pl.semaphore_wait(barrier, CHIPS)

    def ask(step, carry):
        to, device = place(step)
        pltpu.make_async_remote_copy(
            src_ref=slots_ref, dst_ref=requests.at[chip], send_sem=request_send,
            recv_sem=request_sem, device_id=device, device_id_type=MESH,
        ).start()
        return carry

    lax.fori_loop(1, CHIPS, ask, 0)
    pairs = [
        pltpu.make_async_remote_copy(
            src_ref=array.at[core], dst_ref=array.at[core], send_sem=pair_send.at[n],
            recv_sem=pair_recv.at[n], device_id=other, device_id_type=MESH,
        )
        for n, array in enumerate((duals, limits))
    ]
    for copy in pairs:
        copy.start()
    requests[chip] = slots_ref[...]

    for b in range(MEMBER_BLOCKS):
        usage = usage_ref[:, b * WIDTH : (b + 1) * WIDTH]
        high, low = split(usage)
        stacked = jnp.concatenate([high, high, low, low], axis=0).astype(F32)
        left[b, :, 0:32] = stacked.T.astype(BF16)
        right[b] = jnp.concatenate([high * 2, low * 2], axis=0)

    rest = requests.at[pl.ds(0, CHIPS - 1)]
    pltpu.make_async_copy(rest, rest, request_sem).wait()
    table = pltpu.make_async_copy(requests, wanted, want_sem)
    table.start()
    for copy in pairs:
        copy.wait()
    table.wait()

    def sort_tiles():
        square = (TILES, TILES)
        down = lax.broadcasted_iota(jnp.int32, square, 0)
        across = lax.broadcasted_iota(jnp.int32, square, 1)

        def column(row):
            return jnp.broadcast_to(row, square).T

        def placed(chosen, numbers):
            return jnp.sum(jnp.where(chosen, numbers, 0), axis=0, keepdims=True)

        given = slot_ref[...]
        slot = given // 32 * 32 + given % 16 * 2 + given // 16 % 2
        slots = column(slot)
        before = (slots < slot) | ((slots == slot) & (down < across))
        rank = column(placed(before, 1))
        at = rank == across
        order = placed(at, down)
        panels = placed(at, slots)
        earlier = placed(rank == across - 1, slots)
        members = placed(at, column(place_ref[...]))
        last = jnp.maximum(placed(slots <= across, 1) - 1, 0)
        lane = lax.broadcasted_iota(jnp.int32, (1, TILES), 1)
        real = order < count_ref[0]
        counted = jnp.where(real, members, -1)
        whole[...] = jnp.zeros_like(whole)
        parts[...] = jnp.zeros_like(parts)
        for n, row in enumerate((order, panels, members, last, counted)):
            whole[n : n + 1, :] = row
        parts[0:1, :] = jnp.where((panels == earlier) & (lane > 0), 1.0, 0.0)
        parts[1:2, :] = jnp.where(real, 1.0, 0.0)
        tables = [
            pltpu.make_async_copy(source, target, input_sem.at[n])
            for n, (source, target) in enumerate(((whole, whole_smem), (parts, parts_smem)))
        ]
        for copy in tables:
            copy.start()
        for copy in tables:
            copy.wait()

    owners = [(lax.div(mem, 2) * 2 + q) * ITEM_AXIS + item for q in range(2)]

    def want(of, q):
        return wanted[of, 0, owners[q]] - owners[q] * BLOCKS

    def duals_copy(it, h, step):
        to, device = place(step)
        return pltpu.make_async_remote_copy(
            src_ref=dual_out.at[it, h, to], dst_ref=dual_in[it][h].at[chip],
            send_sem=dual_send.at[it, h], recv_sem=dual_recv.at[it, h],
            device_id=device, device_id_type=MESH,
        )

    def loads_copy(it, h, step):
        to, device = place(step)
        return pltpu.make_async_remote_copy(
            src_ref=load_out.at[it, h, to], dst_ref=load_in.at[it, h, chip],
            send_sem=load_send.at[it, h], recv_sem=load_recv.at[it, h],
            device_id=device, device_id_type=MESH,
        )

    def pick(h, to, q):
        return duals[q, h, jnp.maximum(want(to, q), 0)]

    def send_duals(it, h):
        def one(step, carry):
            send_dual(it, h, step)
            return carry

        lax.fori_loop(1, CHIPS, one, 0, unroll=3)
        keep_duals(it, h)

    def send_dual(it, h, step):
        to, _ = place(step)
        for q in range(2):
            dual_out[it, h, to, q] = pick(h, to, q)
        duals_copy(it, h, step).start()

    def keep_duals(it, h):
        for q in range(2):
            dual_in[it][h][chip, q] = pick(h, chip, q)

    def send_load(it, h, step):
        to, _ = place(step)
        for q in range(2):
            load_out[it, h, to, q] = prefix[h, whole_smem[3, to * 2 + q]]
        loads_copy(it, h, step).start()

    def keep_load(it, h):
        for q in range(2):
            load_in[it, h, chip, q] = prefix[h, whole_smem[3, chip * 2 + q]]

    def send_loads(it, h):
        def one(step, carry):
            send_load(it, h, step)
            return carry

        lax.fori_loop(1, CHIPS, one, 0, unroll=3)
        keep_load(it, h)

    def arrived(ref, sem):
        rest = ref.at[pl.ds(0, CHIPS - 1)]
        pltpu.make_async_copy(rest, rest, sem).wait()

    def panel(it, h, slot):
        block = dual_in[it][h][slot // 2, slot % 2]
        high = block.astype(BF16).astype(F32)
        pair = jnp.concatenate([high, block - high], axis=0).astype(BF16)
        return jnp.concatenate([pair, pair], axis=0)

    def sweep(it, h):
        def step(group, total):
            for n in range(GROUP):
                t = group * GROUP + n
                block = whole_smem[2, t]
                charge = jnp.dot(
                    left[block, :, 0:32], panel(it, h, whole_smem[1, t]), preferred_element_type=F32
                )
                value = values[whole_smem[0, t], :, h * HALF : (h + 1) * HALF].astype(F32)
                chosen = jnp.clip(value - charge, 0.0, 0.5)
                high, low = split(chosen)
                usage = right[block]
                load = jnp.dot(usage, high, preferred_element_type=F32) + jnp.dot(
                    usage, low, preferred_element_type=F32
                )
                load = load[0:FAMILIES] + load[FAMILIES:]
                total = total * parts_smem[0, t] + load * parts_smem[1, t]
                prefix[h, t] = total
            return total

        lax.fori_loop(0, TILES // GROUP, step, jnp.zeros((FAMILIES, HALF), F32), unroll=8)

    def note_asked():
        rows = lax.broadcasted_iota(jnp.int32, (BLOCKS, HALF), 0)

        def one(step, carry):
            for n in range(4):
                for q in range(2):
                    of = step * 4 + n
                    asked[of, q] = jnp.where(rows == want(of, q), 1.0, 0.0)
            return carry

        lax.fori_loop(0, CHIPS // 4, one, 0)

    def gather_loads(it, h):
        arrived(load_in.at[it, h], load_recv.at[it, h])

        def one(step, sums):
            sums = list(sums)
            for n in range(2):
                of = step * 2 + n
                for q in range(2):
                    piece = load_in[it, h, of, q]
                    for b in range(BLOCKS):
                        sums[q * BLOCKS + b] += piece * asked[of, q, b : b + 1, :]
            return tuple(sums)

        zero = jnp.zeros((FAMILIES, HALF), F32)
        sums = lax.fori_loop(0, CHIPS // 2, one, (zero,) * (2 * BLOCKS), unroll=4)
        for q in range(2):
            for b in range(BLOCKS):
                partial[it, h, q, b] = sums[q * BLOCKS + b]

    def pair_copy(it, h):
        n = 2 + it * 2 + h
        return pltpu.make_async_remote_copy(
            src_ref=partial.at[it, h], dst_ref=partner.at[it, h], send_sem=pair_send.at[n],
            recv_sem=pair_recv.at[n], device_id=other, device_id_type=MESH,
        )

    def ascend(it, h):
        for q in range(2):
            for b in range(BLOCKS):
                slack = partial[it, h, q, b] + partner[it, h, q, b] - limits[q, h, b]
                duals[q, h, b] = jnp.maximum(duals[q, h, b] + ascent_rate * slack, 0.0)

    def finish(it, h):
        for b in range(BLOCKS):
            columns = pl.ds(b * WIDTH + h * HALF, HALF)
            slack = partial[it, h, core, b] + partner[it, h, core, b] - limits[core, h, b]
            slack_ref[:, columns] = slack
            final_ref[:, columns] = jnp.maximum(duals[core, h, b] + ascent_rate * slack, 0.0)

    def worth_sweep(it):
        worths[...] = jnp.zeros_like(worths)
        lanes = lax.broadcasted_iota(jnp.int32, (WIDTH, HALF), 1)

        def step(group, carry):
            total = worths[...]
            for n in range(MEMBER_GROUP):
                t = group * MEMBER_GROUP + n
                block = whole_smem[2, t]
                slot = whole_smem[1, t]
                both = jnp.concatenate([panel(it, 0, slot), panel(it, 1, slot)], axis=1)
                charge = jnp.dot(left[block, :, 0:32], both, preferred_element_type=F32)
                value = values[whole_smem[0, t]].astype(F32)
                worth = value * jnp.clip(value - charge, 0.0, 0.5)
                worth = jnp.sum(worth[:, :HALF] + worth[:, HALF:], axis=1, keepdims=True)
                total += jnp.where(lanes == whole_smem[4, t], worth, 0.0)
            worths[...] = total
            return carry

        lax.fori_loop(0, TILES // MEMBER_GROUP, step, 0, unroll=4)
        rows = worths[...].T[0:MEMBER_BLOCKS] * (2.0 / WIDTH)
        for b in range(MEMBER_BLOCKS):
            for h in range(2):
                worth_ref[2 * b + h : 2 * b + h + 1, :] = rows[b : b + 1, h * HALF : (h + 1) * HALF]

    send_duals(0, 0)
    send_duals(0, 1)
    sort_tiles()
    note_asked()
    value_copy.wait()
    for it in range(ITERS):
        final = it == ITERS - 1
        for h in range(2):
            arrived(dual_in[it][h], dual_recv.at[it, h])
            sweep(it, h)
            if h == 0:
                send_loads(it, h)
        for h in range(2):
            gather_loads(it, h)
            copy = pair_copy(it, h)
            copy.start()
            if h == 0:
                send_loads(it, 1)
            copy.wait()
            if final:
                finish(it, h)
            else:
                ascend(it, h)
                send_duals(it + 1, h)
            if final and h == 0:
                worth_sweep(it)

    sent = requests.at[pl.ds(0, CHIPS - 1)]
    pltpu.make_async_copy(sent, sent, request_send).wait()
    for it in range(ITERS):
        for h in range(2):
            for ref, sem in ((dual_out, dual_send), (load_out, load_send)):
                arrived(ref.at[it, h], sem.at[it, h])


def on_device(
    value_tiles, member_usage, item_duals, capacity, tile_slot, slot_item, real_tile_count, tile_member
):
    vmem = pl.BlockSpec(memory_space=pltpu.VMEM)
    dma = pltpu.SemaphoreType.DMA
    blocks = (FAMILIES, HALF)
    final, slack, worth = pl.pallas_call(
        kernel,
        out_shape=(
            jax.ShapeDtypeStruct(item_duals.shape, F32),
            jax.ShapeDtypeStruct(item_duals.shape, F32),
            jax.ShapeDtypeStruct((2 * MEMBER_BLOCKS, HALF), F32),
        ),
        in_specs=[pl.BlockSpec(memory_space=pltpu.SMEM)] + [pl.BlockSpec(memory_space=pl.ANY)] * 7,
        out_specs=(vmem,) * 3,
        scratch_shapes=[
            pltpu.VMEM((TILES, WIDTH, WIDTH), BF16),
            pltpu.VMEM(member_usage.shape, F32),
            pltpu.VMEM(item_duals.shape, F32),
            pltpu.VMEM(item_duals.shape, F32),
            pltpu.VMEM((1, TILES), jnp.int32),
            pltpu.VMEM((1, TILES), jnp.int32),
            pltpu.VMEM((1, TILES), jnp.int32),
            pltpu.VMEM((8, TILES), jnp.int32),
            pltpu.VMEM((8, TILES), F32),
            pltpu.SMEM((8, TILES), jnp.int32),
            pltpu.SMEM((8, TILES), F32),
            pltpu.VMEM((MEMBER_BLOCKS, WIDTH, HALF), BF16),
            pltpu.VMEM((MEMBER_BLOCKS, 2 * FAMILIES, WIDTH), BF16),
            pltpu.VMEM((2, 2, BLOCKS) + blocks, F32),
            pltpu.VMEM((2, 2, BLOCKS) + blocks, F32),
            pltpu.VMEM((CHIPS, 1, TILES), jnp.int32),
            pltpu.SMEM((CHIPS, 1, TILES), jnp.int32),
            pltpu.VMEM((ITERS, 2, CHIPS, 2) + blocks, F32),
            *[pltpu.VMEM((CHIPS, 2) + blocks, F32)] * (2 * ITERS),
            pltpu.VMEM((ITERS, 2, CHIPS, 2) + blocks, F32),
            pltpu.VMEM((ITERS, 2, CHIPS, 2) + blocks, F32),
            pltpu.VMEM((2, TILES) + blocks, F32),
            pltpu.VMEM((ITERS, 2, 2, BLOCKS) + blocks, F32),
            pltpu.VMEM((ITERS, 2, 2, BLOCKS) + blocks, F32),
            pltpu.VMEM((WIDTH, HALF), F32),
            pltpu.VMEM((CHIPS, 2, BLOCKS, HALF), F32),
            dma, dma((6,)), dma, dma, dma, dma((2 + 2 * ITERS,)), dma((2 + 2 * ITERS,)),
            dma((ITERS, 2)), dma((ITERS, 2)), dma((ITERS, 2)), dma((ITERS, 2)),
        ],
        compiler_params=pltpu.CompilerParams(
            collective_id=0, has_side_effects=True, vmem_limit_bytes=64 * 2**20 - 2**18
        ),
    )(
        real_tile_count, value_tiles, member_usage, item_duals, capacity,
        tile_slot.reshape(1, TILES), slot_item.reshape(1, TILES), tile_member.reshape(1, TILES),
    )
    return final, slack, worth.reshape(MEMBER_BLOCKS * WIDTH)


def solution(mesh):
    both = ("mem", "item")
    return jax.shard_map(
        on_device,
        mesh=mesh,
        in_specs=(
            P(both, None, None),
            P(None, both),
            P(None, both),
            P(None, both),
            P(both),
            P(both),
            P(both),
            P(both),
        ),
        out_specs=(P(None, both), P(None, both), P(both)),
        check_vma=False,
    )
```
